128 devices in a mesh: edit: 8 (over z, y_hi), seq: 16 (over y_lo, x, core).
Axes of the slice: x: 4, y: 4 (y_hi: 2, y_lo: 2; y = y_hi * 2 + y_lo), z: 4, core: 2. Of those that a mesh axis runs over, the one named last changes fastest.
Arguments:
- projected: bfloat16 [8, 4096, 3, 2048], P('edit', 'seq'), may hold values from -6 to 6
- inject: int32 [8, 16, 16], P('edit', 'seq'), may hold values 0 or 1
- text_kv: bfloat16 [8, 2, 256, 2048], P('edit', None, None, 'seq'), may hold values from -6 to 6
- text_len: int32 [8], P('edit'), may hold values from 64 to 256, as said below
- out_weight: bfloat16 [2048, 3072], replicated, may hold values from -0.125 to 0.125
- gate: float32 [8, 3072], P('edit'), may hold values from 1 to 8
Outputs:
- branch_out: bfloat16 [8, 4096, 3072], P('edit', 'seq')
The draws below stay inside these ranges and needn't reach their ends.
Inputs may be any that keep to these rules, and one draw needn't show every extreme that they name: `text_len`: in every draw some prompt has all 256 text tokens.
All inputs are finite; a program needn't handle non-finite values. No bound on the sum of `inject` on one device may be relied on, other than what follows from the above.
Results may differ from the reference program's by a relative error of at most 0.0057.
Values may be sent and summed in bfloat16 or wider, within the bound.
A program may use at most 128 MiB of HBM per device.

```python
import math
import jax
import jax.numpy as jnp
from jax import lax

D = 3072
H = 16
HD = 128
TEXT = 256
TOK_DEV = 256
TOKENS = 4096
CLIPS = 8
HH = 2048
N_SEQ = 16


def draw_projected(key, part):
    key = jax.random.fold_in(key, 11)
    first_key = jax.random.fold_in(key, 0)
    shape = (CLIPS, TOKENS, 3, H * HD)
    noise = jnp.clip(jax.random.normal(first_key, shape, jnp.float32) * 1.41, -6.0, 6.0)
    return noise.astype(jnp.bfloat16)


def draw_text_len(key, part):
    key = jax.random.fold_in(key, 23)
    first_key, second_key = jax.random.split(key)
    lengths = jax.random.randint(first_key, (CLIPS,), TEXT // 4, TEXT + 1)
    chosen = jax.random.randint(second_key, (), 0, CLIPS)
    return jnp.where(jnp.arange(CLIPS) == chosen, TEXT, lengths).astype(jnp.int32)


def with_ends(array, own_key, least, largest):
    place = [jax.random.randint(jax.random.fold_in(own_key, axis), (), 0, length) for axis, length in enumerate(array.shape)]
    widest = array.shape.index(max(array.shape))
    beside = place[:widest] + [(place[widest] + 1) % array.shape[widest]] + place[widest + 1:]
    return array.at[tuple(place)].set(least).at[tuple(beside)].set(largest)


def shard_levels(own_key, dims, cuts, smallest, largest):
    factor_of, own = 1.0, jax.random.fold_in(own_key, 6)
    for axis_at, blocks in cuts:
        heights = jnp.exp(jax.random.uniform(jax.random.fold_in(own, axis_at), (blocks,), jnp.float32, smallest / len(cuts), largest / len(cuts)))
        factor_of = factor_of * jnp.repeat(heights, dims[axis_at] // blocks).reshape([-1 if axis == axis_at else 1 for axis in range(len(dims))])
    return factor_of


def centred(key, extent, deviation, reach, cuts=(), kind=jnp.bfloat16):
    array = deviation * jax.random.normal(key, extent, jnp.float32)
    if cuts:
        array = array * shard_levels(key, extent, cuts, -0.22, 0.18)
    return jnp.clip(array, -reach, reach).astype(kind)


def setup_inputs(seed: int = 0) -> dict:
    key_list = jax.random.split(jax.random.key(seed), 7)
    projected = draw_projected(jax.random.fold_in(key_list[6], 71), 0)
    inject = with_ends((jax.random.randint(key_list[1], (CLIPS, H, N_SEQ), 0, 2) < 1).astype(jnp.int32), jax.random.fold_in(key_list[1], 1), 0, 1)
    text_kv = centred(key_list[2], (CLIPS, 2, TEXT, HH), 1.41, 6.0, ((0, 8), (3, 16)))
    text_len = draw_text_len(jax.random.fold_in(key_list[6], 71), 0)
    out_weight = centred(key_list[4], (HH, D), HH ** -0.5, 0.125)
    gate = jnp.clip(jnp.exp(math.log(8.0) - 2.0794415 * jax.random.uniform(key_list[5], (CLIPS, D), jnp.float32) ** shard_levels(key_list[5], (CLIPS, D), ((0, 8),), -0.2, 0.2)), 1.0, 8.0)
    return dict(projected=projected, inject=inject, text_kv=text_kv, text_len=text_len, out_weight=out_weight, gate=gate)


def reference(projected, inject, text_kv, text_len, out_weight, gate):
    score_scale = 1.0 / math.sqrt(HD)
    source = projected[0, :, 1:3].reshape(TOKENS, 2, H, HD)

    def one_clip(clip_items):
        clip_data, mask_rows, text_pairs, length, gain_row = clip_items
        mask_tokens = jnp.repeat(mask_rows, TOK_DEV, axis=1)
        chosen = (mask_tokens.T == 1)[:, None, :, None]
        own_pairs = clip_data[:, 1:3].reshape(TOKENS, 2, H, HD)
        pairs = jnp.where(chosen, source, own_pairs)
        text_split = text_pairs.reshape(2, TEXT, H, HD)
        key_rows = jnp.concatenate([pairs[:, 0], text_split[0]], axis=0)
        value_rows = jnp.concatenate([pairs[:, 1], text_split[1]], axis=0)
        queries = clip_data[:, 0].reshape(TOKENS, H, HD)
        usable = jnp.concatenate([jnp.ones((TOKENS,), bool), jnp.arange(TEXT) < length])

        def one_head(head_items):
            query, keys_h, values_h = head_items
            scores = jnp.dot(query, keys_h.T, preferred_element_type=jnp.float32) * score_scale
            scores = jnp.where(usable[None, :], scores, -jnp.inf)
            top_score = lax.optimization_barrier(jnp.max(scores, axis=1, keepdims=True))
            expo = jnp.exp(scores - top_score)
            weights = (expo / lax.optimization_barrier(jnp.sum(expo, axis=1, keepdims=True))).astype(jnp.bfloat16)
            return jnp.dot(weights, values_h, preferred_element_type=jnp.float32).astype(jnp.bfloat16)
        attended = lax.map(one_head, (queries.transpose(1, 0, 2), key_rows.transpose(1, 0, 2), value_rows.transpose(1, 0, 2)))
        flat_heads = attended.transpose(1, 0, 2).reshape(TOKENS, H * HD)
        result = jnp.dot(flat_heads, out_weight, preferred_element_type=jnp.float32) * gain_row[None, :]
        return result.astype(jnp.bfloat16)
    return lax.map(one_clip, (projected, inject, text_kv, text_len, gate))
```

```python
import functools
import math

import jax
import jax.numpy as jnp
from jax import lax
from jax.experimental import pallas as pl
from jax.experimental.pallas import tpu as pltpu
from jax.sharding import PartitionSpec as P

MESH = pl.DeviceIdType.MESH
CONTRACT_LAST = (((1,), (1,)), ((), ()))
LANES = 128


def kernel(
    pieces, edits, ring,
    proj, inj, text, text_len, weight, gate, out,
    own, src, sel, queries, kv, inj_own, inj_all, mask_row,
    s_a, s_b, m_a, m_b, rows_out, cols_out, weight_here,
    load_sem, src_sem, text_sem, weight_sem, inj_send, inj_recv, q_send, q_recv,
    cast_send, cast_recv, kv_send, kv_recv, o_send, o_recv,
):
    e = lax.axis_index("edit")
    me = lax.axis_index("seq")
    z, half = e // 2, e % 2
    depth = edits // 2
    block = own.shape[1]
    rows = block // pieces
    group = rows * ring
    total = block * ring
    text_rows = text.shape[1]
    keys = total + text_rows
    root = e == 0

    def peer(d):
        return lax.rem(me + d, ring)

    def columns(head):
        return pl.ds(pl.multiple_of(head * LANES, LANES), LANES)

    load_own = pltpu.make_async_copy(proj.at[pl.ds(1, 2)], own, load_sem)
    load_own.start()
    load_src = pltpu.make_async_copy(proj.at[pl.ds(1, 2)], src, src_sem)

    @pl.when(root)
    def _():
        load_src.start()

    load_text = pltpu.make_async_copy(
        text, kv.at[:, pl.ds(total, text_rows), pl.ds(0, LANES)], text_sem
    )
    load_text.start()
    load_weight = pltpu.make_async_copy(weight, weight_here, weight_sem)

    barrier = pltpu.get_barrier_semaphore()

    def greet(d, carry):
        pl.semaphore_signal(barrier, inc=1, device_id=(e, peer(d)), device_id_type=MESH)
        return carry

    lax.fori_loop(1, ring, greet, 0)
    up, down = lax.rem(z + 1, depth), lax.rem(z + depth - 1, depth)
    for other in (up * 2 + half, down * 2 + half, z * 2 + 1 - half):
        pl.semaphore_signal(barrier, inc=1, device_id=(other, me), device_id_type=MESH)
    inj_own[...] = jnp.zeros_like(inj_own)
    inj_own[0:1, 0:ring] = inj[...]
    kv[1, :, LANES:] = jnp.ones((keys, LANES), jnp.bfloat16)
    pl.semaphore_wait(barrier, ring - 1 + 3)

    def inj_copy(d):
        return pltpu.make_async_remote_copy(
            inj_own, inj_all.at[me], inj_send, inj_recv, (e, peer(d)), MESH
        )

    def q_copy(d):
        there = peer(d)
        return pltpu.make_async_remote_copy(
            proj.at[0, :, columns(there)],
            queries.at[pl.ds(pl.multiple_of(me * block, block), block)],
            q_send, q_recv, (e, there), MESH,
        )

    def each(first, last, action):
        def step(d, carry):
            action(d)
            return carry

        lax.fori_loop(first, last, step, 0)

    each(1, ring, lambda d: inj_copy(d).start())
    own_inj = pltpu.make_async_copy(inj_own, inj_all.at[me], inj_recv)
    own_inj.start()
    own_q = pltpu.make_async_copy(
        proj.at[0, :, columns(me)],
        queries.at[pl.ds(pl.multiple_of(me * block, block), block)],
        q_recv,
    )
    own_q.start()

    def cast_sends(k):
        odd = lax.rem(k, 2)
        key_from = lax.rem(z - odd + depth, depth)
        value_from = lax.rem(depth - 1 - odd - z + depth, depth)
        first, second = half == 0, half == 1
        return (
            (jnp.logical_or(jnp.logical_and(first, z < depth - 1), jnp.logical_and(second, key_from <= 1)),
             0, up * 2 + half),
            (jnp.logical_or(jnp.logical_and(first, z == odd), jnp.logical_and(second, key_from == 0)),
             0, lax.rem(z + (depth - 1) * half, depth) * 2 + 1),
            (jnp.logical_or(jnp.logical_and(first, z != 1), jnp.logical_and(second, value_from <= 1)),
             1, down * 2 + half),
            (jnp.logical_or(jnp.logical_and(first, z == depth - 1 - odd), jnp.logical_and(second, value_from == 0)),
             1, lax.rem(z + half, depth) * 2 + 1),
        )

    def piece_rows(k):
        return pl.ds(pl.multiple_of(k * rows, rows), rows)

    def cast_copy(k, role, part, there):
        here = src.at[part, piece_rows(k)]
        return pltpu.make_async_remote_copy(
            here, here, cast_send.at[role, k], cast_recv.at[part, k], (there, me), MESH
        )

    def kv_rows(k, owner):
        return pl.ds(pl.multiple_of(k * group + owner * rows, rows), rows)

    def kv_copy(k, d):
        there = peer(d)
        return pltpu.make_async_remote_copy(
            sel.at[:, piece_rows(k), columns(there)],
            kv.at[:, kv_rows(k, me), pl.ds(0, LANES)],
            kv_send.at[k], kv_recv.at[k], (e, there), MESH,
        )

    def own_kv_copy(k):
        return pltpu.make_async_copy(
            sel.at[:, piece_rows(k), columns(me)],
            kv.at[:, kv_rows(k, me), pl.ds(0, LANES)],
            kv_recv.at[k],
        )

    @pl.when(root)
    def _():
        load_src.wait()

    load_own.wait()
    pltpu.make_async_copy(inj_all, inj_all, inj_recv).wait()
    lane = lax.broadcasted_iota(jnp.int32, (1, LANES), 1)
    for head in range(ring):
        mine = jnp.where(lane == me, inj_all[head, 0:1, :], 0)
        taken = jnp.sum(mine, axis=1, keepdims=True)
        mask_row[:, head * LANES : (head + 1) * LANES] = jnp.broadcast_to(taken, (8, LANES))

    q_step = -(-(ring - 1) // pieces)

    def send_piece(k, carry):
        for part in range(2):

            @pl.when(jnp.logical_not(root))
            def _():
                cast_copy(k, 0, part, e).wait_recv()

            for role, (wanted, moved, there) in enumerate(cast_sends(k)):
                if moved == part:

                    @pl.when(wanted)
                    def _(role=role, there=there):
                        cast_copy(k, role, part, there).start()

        here = piece_rows(k)
        taken = mask_row[0:1, :] == 1
        for part in range(2):
            sel[part, here, :] = jnp.where(
                taken, src[part, here, :].astype(jnp.float32), own[part, here, :].astype(jnp.float32)
            ).astype(jnp.bfloat16)
        each(1, ring, lambda d: kv_copy(k, d).start())
        own_kv_copy(k).start()
        for extra in range(q_step):
            d = k * q_step + 1 + extra

            @pl.when(d < ring)
            def _(d=d):
                q_copy(d).start()

        return carry

    lax.fori_loop(0, pieces, send_piece, 0)
    load_weight.start()

    load_text.wait()
    pltpu.make_async_copy(queries, queries, q_recv).wait()

    def await_piece(k, carry):
        part = kv.at[:, pl.ds(pl.multiple_of(k * group, group), group), pl.ds(0, LANES)]
        pltpu.make_async_copy(part, part, kv_recv.at[k]).wait()
        return carry

    lax.fori_loop(0, pieces, await_piece, 0)

    scale = math.log2(math.e) / math.sqrt(LANES)
    chunk = text_rows
    usable = lax.broadcasted_iota(jnp.int32, (1, chunk), 1) < text_len[0]
    scores, tops = (s_a, s_b), (m_a, m_b)

    def at(i):
        owner = lax.rem(me + 1 + i, ring)
        return owner, pl.ds(pl.multiple_of(owner * block, block), block)

    def o_copy(i):
        owner, here = at(i)
        return pltpu.make_async_remote_copy(
            rows_out.at[here], cols_out.at[:, columns(me)], o_send, o_recv, (e, owner), MESH
        )

    def attend(i, slot, first=False, last=False):
        other = 1 - slot
        if not last:
            query = queries[at(i)[1], :]
        if not first:
            top = tops[other][:, 0:1]
        highest, total_out = None, None
        for j in range(keys // chunk):
            here = slice(j * chunk, (j + 1) * chunk)
            if not last:
                s = lax.dot_general(
                    query, kv[0, here, 0:LANES], CONTRACT_LAST, preferred_element_type=jnp.float32
                )
                if j == keys // chunk - 1:
                    s = jnp.where(usable, s, -1e30)
                scores[slot][:, here] = s
                for c in range(chunk // LANES):
                    part = s[:, c * LANES : (c + 1) * LANES]
                    highest = part if highest is None else jnp.maximum(highest, part)
            if not first:
                p = jnp.exp2(scores[other][:, here] * scale - top).astype(jnp.bfloat16)
                part = jnp.dot(p, kv[1, here, :], preferred_element_type=jnp.float32)
                total_out = part if total_out is None else total_out + part
        if not last:
            tops[slot][...] = jnp.broadcast_to(
                jnp.max(highest, axis=1, keepdims=True) * scale, (block, LANES)
            )
        if not first:
            result = total_out[:, :LANES] / total_out[:, LANES : LANES + 1]
            rows_out[at(i - 1)[1], :] = result.astype(jnp.bfloat16)

    def two(h, carry):
        attend(2 * h + 1, 1)
        o_copy(2 * h).start()
        attend(2 * h + 2, 0)
        o_copy(2 * h + 1).start()
        return carry

    attend(0, 0, first=True)
    lax.fori_loop(0, (ring - 2) // 2, two, 0)
    attend(ring - 1, 1)
    o_copy(ring - 2).start()
    attend(ring, 0, last=True)
    own_o = pltpu.make_async_copy(rows_out.at[at(ring - 1)[1]], cols_out.at[:, columns(me)], o_recv)
    own_o.start()
    load_weight.wait()
    pltpu.make_async_copy(cols_out, cols_out, o_recv).wait()

    wide = 512 if out.shape[1] % 512 == 0 else LANES

    def project(n, carry):
        here = pl.ds(pl.multiple_of(n * wide, wide), wide)
        result = jnp.dot(cols_out[...], weight_here[:, here], preferred_element_type=jnp.float32)
        out[:, here] = (result * gate[:, here]).astype(jnp.bfloat16)
        return carry

    lax.fori_loop(0, out.shape[1] // wide, project, 0)

    each(1, ring, lambda d: inj_copy(d).wait_send())
    each(1, ring, lambda d: q_copy(d).wait_send())
    each(0, ring - 1, lambda i: o_copy(i).wait_send())

    def finish_piece(k, carry):
        for role, (wanted, part, there) in enumerate(cast_sends(k)):

            @pl.when(wanted)
            def _(role=role, part=part, there=there):
                cast_copy(k, role, part, there).wait_send()

        each(1, ring, lambda d: kv_copy(k, d).wait_send())
        return carry

    lax.fori_loop(0, pieces, finish_piece, 0)


def per_device(pieces, edits, ring, projected, inject, text_kv, text_len, out_weight, gate):
    block, width = projected.shape[1], projected.shape[3]
    text_rows = text_kv.shape[2]
    total = block * ring
    keys = total + text_rows
    wide = out_weight.shape[1]
    bf16, f32, i32 = jnp.bfloat16, jnp.float32, jnp.int32
    vmem = pl.BlockSpec(memory_space=pltpu.VMEM)
    far = pl.BlockSpec(memory_space=pl.ANY)
    dma = pltpu.SemaphoreType.DMA
    result = pl.pallas_call(
        functools.partial(kernel, pieces, edits, ring),
        out_shape=jax.ShapeDtypeStruct((block, wide), bf16),
        in_specs=[far, vmem, far, pl.BlockSpec(memory_space=pltpu.SMEM), far, vmem],
        out_specs=vmem,
        scratch_shapes=[
            pltpu.VMEM((2, block, width), bf16),
            pltpu.VMEM((2, block, width), bf16),
            pltpu.VMEM((2, block, width), bf16),
            pltpu.VMEM((total, LANES), bf16),
            pltpu.VMEM((2, keys, 2 * LANES), bf16),
            pltpu.VMEM((8, LANES), i32),
            pltpu.VMEM((ring, 8, LANES), i32),
            pltpu.VMEM((8, width), i32),
            pltpu.VMEM((block, keys), f32),
            pltpu.VMEM((block, keys), f32),
            pltpu.VMEM((block, LANES), f32),
            pltpu.VMEM((block, LANES), f32),
            pltpu.VMEM((total, LANES), bf16),
            pltpu.VMEM((block, width), bf16),
            pltpu.VMEM(out_weight.shape, bf16),
            dma, dma, dma, dma, dma, dma, dma, dma,
            dma((4, pieces)), dma((2, pieces)), dma((pieces,)), dma((pieces,)),
            dma, dma,
        ],
        compiler_params=pltpu.CompilerParams(
            collective_id=0, has_side_effects=True, vmem_limit_bytes=56 * 2**20
        ),
    )(
        projected[0].transpose(1, 0, 2), inject[0], text_kv[0], text_len, out_weight, gate,
    )
    return result[None]


def solution(mesh):
    edits, ring = mesh.shape["edit"], mesh.shape["seq"]
    return jax.shard_map(
        functools.partial(per_device, 8, edits, ring),
        mesh=mesh,
        in_specs=(
            P("edit", "seq", None, None),
            P("edit", "seq", None),
            P("edit", None, None, "seq"),
            P("edit"),
            P(),
            P("edit", None),
        ),
        out_specs=P("edit", "seq", None),
        check_vma=False,
    )
```

```python
import functools
import math

import jax
import jax.numpy as jnp
from jax import lax
from jax.experimental import pallas as pl
from jax.experimental.pallas import tpu as pltpu
from jax.sharding import PartitionSpec as P

MESH = pl.DeviceIdType.MESH
CONTRACT_LAST = (((1,), (1,)), ((), ()))
LANES = 128
HOP = 2
AHEAD = 3
PIECES = 16


def kernel(
    edits, ring,
    proj, inj, text, text_len, weight, gate, out,
    queries, kv, src, inj_own, inj_here, mask, s_a, s_b, m_a, m_b, rows_out, cols_out, weight_here,
    weight_sem, text_send, text_recv, inj_send, inj_recv, q_send, q_recv,
    cast_send, cast_recv, kv_send, kv_recv, o_send, o_recv,
):
    e = lax.axis_index("edit")
    me = lax.axis_index("seq")
    z, half = e // 2, e % 2
    depth = edits // 2
    block = out.shape[0]
    rows = block // PIECES
    group = rows * ring
    total = block * ring
    text_rows = text.shape[1]
    keys = total + text_rows
    root = e == 0
    swap = ring // 2
    other_row = lax.rem(me + swap, ring)

    def peer(d):
        return lax.rem(me + d, ring)

    def head_of(device):
        return lax.rem(device + swap * half, ring)

    def columns(head):
        return pl.ds(pl.multiple_of(head * LANES, LANES), LANES)

    def each(first, last, action):
        def step(d, carry):
            action(d)
            return carry

        lax.fori_loop(first, last, step, 0)

    load_weight = pltpu.make_async_copy(weight, weight_here, weight_sem)
    load_weight.start()

    barrier = pltpu.get_barrier_semaphore()

    def greet(d):
        pl.semaphore_signal(barrier, inc=1, device_id=(e, peer(d)), device_id_type=MESH)

    each(1, ring, greet)
    up, down = lax.rem(z + 1, depth), lax.rem(z + depth - 1, depth)
    for other in ((up * 2 + half, me), (down * 2 + half, me), (z * 2 + 1 - half, other_row)):
        pl.semaphore_signal(barrier, inc=1, device_id=other, device_id_type=MESH)
    inj_own[...] = jnp.zeros_like(inj_own)
    inj_own[0:1, 0:ring] = inj[...]
    kv[1, :, LANES:] = jnp.ones((keys, LANES), jnp.bfloat16)
    pl.semaphore_wait(barrier, ring - 1 + 3)

    def piece_rows(k):
        return pl.ds(pl.multiple_of(k * rows, rows), rows)

    def group_rows(k):
        return pl.ds(pl.multiple_of(k * group, group), group)

    def landing(k):
        return pl.ds(pl.multiple_of(k * group + me * rows, rows), rows)

    def q_copy(k, d):
        there = peer(d)
        return pltpu.make_async_remote_copy(
            proj.at[0, piece_rows(k), columns(head_of(there))], queries.at[landing(k)],
            q_send, q_recv.at[k], (e, there), MESH,
        )

    def kv_copy(k, d):
        there = peer(d)
        return pltpu.make_async_remote_copy(
            proj.at[pl.ds(1, 2), piece_rows(k), columns(head_of(there))],
            kv.at[:, landing(k), pl.ds(0, LANES)],
            kv_send, kv_recv.at[k], (e, there), MESH,
        )

    def push_q(k):
        each(1, ring, lambda d: q_copy(k, d).start())
        pltpu.make_async_copy(
            proj.at[0, piece_rows(k), columns(head_of(me))], queries.at[landing(k)], q_recv.at[k]
        ).start()

    def push_kv(k):
        each(1, ring, lambda d: kv_copy(k, d).start())
        pltpu.make_async_copy(
            proj.at[pl.ds(1, 2), piece_rows(k), columns(head_of(me))],
            kv.at[:, landing(k), pl.ds(0, LANES)], kv_recv.at[k],
        ).start()

    def await_kv(k):
        here = kv.at[:, group_rows(k), pl.ds(0, LANES)]
        pltpu.make_async_copy(here, here, kv_recv.at[k]).wait()

    def near(distance):
        return distance - 2 * (distance // (depth - 1))

    def apart(part, odd):
        if part == 0:
            return lax.rem(z - odd + depth, depth)
        return lax.rem(2 * depth - odd - z, depth)

    def lag(part, odd):
        straight = z if part == 0 else lax.rem(depth - z, depth)
        return HOP * ((1 - half) * straight + half * (odd + 1 + near(apart(part, odd))))

    def cast_sends(part, odd):
        first, second = half == 0, half == 1
        distance = apart(part, odd)
        onward = z < depth - 1 if part == 0 else z != 1
        cross = z == odd if part == 0 else z == lax.rem(depth - odd, depth)
        back = lax.rem(z + (depth - 1) * half, depth) if part == 0 else lax.rem(z + half, depth)
        ahead = up if part == 0 else down
        return (
            (jnp.logical_or(jnp.logical_and(first, onward), jnp.logical_and(second, distance <= 1)),
             (ahead * 2 + half, me)),
            (jnp.logical_or(jnp.logical_and(first, cross), jnp.logical_and(second, distance == 0)),
             (back * 2 + 1, lax.rem(me + swap * (1 - half), ring))),
        )

    def cast_copy(k, role, part, there, first):
        here = kv.at[part, group_rows(k), pl.ds(0, LANES)] if first else src.at[part, group_rows(k)]
        return pltpu.make_async_remote_copy(
            here, src.at[part, group_rows(k)], cast_send.at[2 * part + role, k],
            cast_recv.at[part, k], there, MESH,
        )

    def cast_start(k, part, odd, first):
        for role, (wanted, there) in enumerate(cast_sends(part, odd)):

            @pl.when(wanted)
            def _(role=role, there=there):
                cast_copy(k, role, part, there, first).start()

    def cast_done(k, part, odd):
        for role, (wanted, there) in enumerate(cast_sends(part, odd)):

            @pl.when(wanted)
            def _(role=role, there=there):
                cast_copy(k, role, part, there, False).wait_send()

    most = HOP * depth

    def cast_step(t, carry):
        for odd in range(2):
            for part in range(2):
                k = t - lag(part, odd)
                here = jnp.logical_and(
                    jnp.logical_and(k >= 0, k < PIECES), lax.rem(k + 2 * most, 2) == odd
                )

                @pl.when(jnp.logical_and(here, root))
                def _(k=k, part=part, odd=odd):
                    if part == 0:
                        await_kv(k)
                    cast_start(k, part, odd, True)

                @pl.when(jnp.logical_and(here, jnp.logical_not(root)))
                def _(k=k, part=part, odd=odd):
                    cast_copy(k, 0, part, (e, me), False).wait_recv()
                    cast_start(k, part, odd, False)

        @pl.when(root)
        def _():
            ahead = t + AHEAD

            @pl.when(ahead < PIECES)
            def _():
                push_kv(ahead)

            @pl.when(jnp.logical_and(ahead >= PIECES, ahead < PIECES + PIECES // 2))
            def _():
                push_q(2 * (ahead - PIECES))
                push_q(2 * (ahead - PIECES) + 1)

        @pl.when(jnp.logical_not(root))
        def _():
            quick = PIECES // 4

            @pl.when(t < quick)
            def _():
                each(4 * t, 4 * t + 4, push_q)

            @pl.when(jnp.logical_and(t >= quick, t < quick + PIECES))
            def _():
                push_kv(t - quick)

        return carry

    @pl.when(root)
    def _():
        each(0, AHEAD, push_kv)

    text_here = kv.at[:, pl.ds(total, text_rows), pl.ds(0, LANES)]
    text_copy = pltpu.make_async_remote_copy(text, text_here, text_send, text_recv, (e, other_row), MESH)
    inj_copy = pltpu.make_async_remote_copy(inj_own, inj_here, inj_send, inj_recv, (e, other_row), MESH)

    @pl.when(half == 1)
    def _():
        inj_copy.start()
        text_copy.start()

    @pl.when(half == 0)
    def _():
        pltpu.make_async_copy(inj_own, inj_here, inj_recv).start()
        pltpu.make_async_copy(text, text_here, text_recv).start()

    lax.fori_loop(0, PIECES + most, cast_step, 0)

    inj_copy.wait_recv()
    text_copy.wait_recv()

    @pl.when(jnp.logical_not(root))
    def _():
        lane = lax.broadcasted_iota(jnp.int32, (1, LANES), 1)
        for owner in range(ring):
            taken = jnp.sum(jnp.where(lane == owner, inj_here[0:1, :], 0), axis=1, keepdims=True)
            mask[owner * rows : (owner + 1) * rows, :] = jnp.broadcast_to(taken, (rows, LANES))

        def choose(k):
            await_kv(k)
            here = group_rows(k)
            for part in range(2):
                kv[part, here, 0:LANES] = jnp.where(
                    mask[...] == 1,
                    src[part, here, :].astype(jnp.float32),
                    kv[part, here, 0:LANES].astype(jnp.float32),
                ).astype(jnp.bfloat16)

        each(0, PIECES, choose)

    scale = math.log2(math.e) / math.sqrt(LANES)
    chunk = text_rows
    usable = lax.broadcasted_iota(jnp.int32, (1, chunk), 1) < text_len[0]
    scores, tops = (s_a, s_b), (m_a, m_b)

    def o_copy(k, d):
        there = peer(d)
        return pltpu.make_async_remote_copy(
            rows_out.at[pl.ds(pl.multiple_of(k * group + there * rows, rows), rows)],
            cols_out.at[piece_rows(k), columns(head_of(me))],
            o_send, o_recv, (e, there), MESH,
        )

    def push_o(k):
        each(1, ring, lambda d: o_copy(k, d).start())
        pltpu.make_async_copy(
            rows_out.at[landing(k)], cols_out.at[piece_rows(k), columns(head_of(me))], o_recv
        ).start()

    def attend(i, slot, first=False, last=False):
        other = 1 - slot
        if not last:
            here = queries.at[group_rows(i)]
            pltpu.make_async_copy(here, here, q_recv.at[i]).wait()
            query = queries[group_rows(i), :]
        if not first:
            top = tops[other][:, 0:1]
        highest, total_out = None, None
        for j in range(keys // chunk):
            here = slice(j * chunk, (j + 1) * chunk)
            if not last:
                s = lax.dot_general(
                    query, kv[0, here, 0:LANES], CONTRACT_LAST, preferred_element_type=jnp.float32
                )
                if j == keys // chunk - 1:
                    s = jnp.where(usable, s, -1e30)
                scores[slot][:, here] = s
                for c in range(chunk // LANES):
                    part = s[:, c * LANES : (c + 1) * LANES]
                    highest = part if highest is None else jnp.maximum(highest, part)
            if not first:
                p = jnp.exp2(scores[other][:, here] * scale - top).astype(jnp.bfloat16)
                part = jnp.dot(p, kv[1, here, :], preferred_element_type=jnp.float32)
                total_out = part if total_out is None else total_out + part
        if not last:
            tops[slot][...] = jnp.broadcast_to(
                jnp.max(highest, axis=1, keepdims=True) * scale, (group, LANES)
            )
        if not first:
            result = total_out[:, :LANES] / total_out[:, LANES : LANES + 1]
            rows_out[group_rows(i - 1), :] = result.astype(jnp.bfloat16)

    def two(h):
        attend(2 * h + 1, 1)
        push_o(2 * h)
        attend(2 * h + 2, 0)
        push_o(2 * h + 1)

    attend(0, 0, first=True)
    each(0, (PIECES - 2) // 2, two)
    attend(PIECES - 1, 1)
    push_o(PIECES - 2)
    attend(PIECES, 0, last=True)
    push_o(PIECES - 1)
    load_weight.wait()
    pltpu.make_async_copy(cols_out, cols_out, o_recv).wait()

    wide = 512 if out.shape[1] % 512 == 0 else LANES

    def project(n):
        here = pl.ds(pl.multiple_of(n * wide, wide), wide)
        result = jnp.dot(cols_out[...], weight_here[:, here], preferred_element_type=jnp.float32)
        out[:, here] = (result * gate[:, here]).astype(jnp.bfloat16)

    each(0, out.shape[1] // wide, project)

    @pl.when(half == 1)
    def _():
        inj_copy.wait_send()
        text_copy.wait_send()

    def finish_piece(k):
        for odd in range(2):

            @pl.when(lax.rem(k, 2) == odd)
            def _(odd=odd):
                for part in range(2):
                    cast_done(k, part, odd)

        each(1, ring, lambda d: q_copy(k, d).wait_send())
        each(1, ring, lambda d: kv_copy(k, d).wait_send())
        each(1, ring, lambda d: o_copy(k, d).wait_send())

    each(0, PIECES, finish_piece)


def per_device(edits, ring, projected, inject, text_kv, text_len, out_weight, gate):
    block, width = projected.shape[1], projected.shape[3]
    text_rows = text_kv.shape[2]
    total = block * ring
    keys = total + text_rows
    group = total // PIECES
    bf16, f32, i32 = jnp.bfloat16, jnp.float32, jnp.int32
    vmem = pl.BlockSpec(memory_space=pltpu.VMEM)
    far = pl.BlockSpec(memory_space=pl.ANY)
    dma = pltpu.SemaphoreType.DMA
    result = pl.pallas_call(
        functools.partial(kernel, edits, ring),
        out_shape=jax.ShapeDtypeStruct((block, out_weight.shape[1]), bf16),
        in_specs=[far, vmem, far, pl.BlockSpec(memory_space=pltpu.SMEM), far, vmem],
        out_specs=vmem,
        scratch_shapes=[
            pltpu.VMEM((total, LANES), bf16),
            pltpu.VMEM((2, keys, 2 * LANES), bf16),
            pltpu.VMEM((2, total, LANES), bf16),
            pltpu.VMEM((8, LANES), i32),
            pltpu.VMEM((8, LANES), i32),
            pltpu.VMEM((group, LANES), i32),
            pltpu.VMEM((group, keys), f32),
            pltpu.VMEM((group, keys), f32),
            pltpu.VMEM((group, LANES), f32),
            pltpu.VMEM((group, LANES), f32),
            pltpu.VMEM((total, LANES), bf16),
            pltpu.VMEM((block, width), bf16),
            pltpu.VMEM(out_weight.shape, bf16),
            dma, dma, dma, dma, dma, dma, dma((PIECES,)),
            dma((4, PIECES)), dma((2, PIECES)), dma, dma((PIECES,)), dma, dma,
        ],
        compiler_params=pltpu.CompilerParams(
            collective_id=0, has_side_effects=True, vmem_limit_bytes=56 * 2**20
        ),
    )(
        projected[0].transpose(1, 0, 2), inject[0], text_kv[0], text_len, out_weight, gate,
    )
    return result[None]


def solution(mesh):
    return jax.shard_map(
        functools.partial(per_device, mesh.shape["edit"], mesh.shape["seq"]),
        mesh=mesh,
        in_specs=(
            P("edit", "seq", None, None),
            P("edit", "seq", None),
            P("edit", None, None, "seq"),
            P("edit"),
            P(),
            P("edit", None),
        ),
        out_specs=P("edit", "seq", None),
        check_vma=False,
    )
```

```python
import functools
import math

import jax
import jax.numpy as jnp
from jax import lax
from jax.experimental import pallas as pl
from jax.experimental.pallas import tpu as pltpu
from jax.sharding import PartitionSpec as P

MESH = pl.DeviceIdType.MESH
CONTRACT_LAST = (((1,), (1,)), ((), ()))
LANES = 128
HOP = 2
AHEAD = 3
PIECES = 16


def kernel(
    edits, ring,
    proj, inj, text, text_len, weight, gate, out,
    queries, kv, text_kv, src, inj_own, inj_here, mask, s_a, s_b, m_a, m_b, rows_out, cols_out, weight_here,
    early_out, early_top, weight_sem, text_send, text_recv, inj_send, inj_recv, q_send, q_recv,
    cast_send, cast_recv, kv_send, kv_recv, o_send, o_recv,
):
    e = lax.axis_index("edit")
    me = lax.axis_index("seq")
    z, half = e // 2, e % 2
    depth = edits // 2
    rows = proj.shape[2]
    group = rows * ring
    root = e == 0
    swap = ring // 2
    other_row = lax.rem(me + swap, ring)

    def peer(d):
        return lax.rem(me + d, ring)

    def head_of(device):
        return lax.rem(device + swap * half, ring)

    def columns(head):
        return pl.ds(pl.multiple_of(head * LANES, LANES), LANES)

    def each(first, last, action):
        def step(d, carry):
            action(d)
            return carry

        lax.fori_loop(first, last, step, 0)

    load_weight = pltpu.make_async_copy(weight, weight_here, weight_sem)
    load_weight.start()

    barrier = pltpu.get_barrier_semaphore()

    def greet(d):
        pl.semaphore_signal(barrier, inc=1, device_id=(e, peer(d)), device_id_type=MESH)

    each(1, ring, greet)
    up, down = lax.rem(z + 1, depth), lax.rem(z + depth - 1, depth)
    for other in ((up * 2 + half, me), (down * 2 + half, me), (z * 2 + 1 - half, other_row)):
        pl.semaphore_signal(barrier, inc=1, device_id=other, device_id_type=MESH)
    inj_own[...] = jnp.zeros_like(inj_own)
    inj_own[0:1, 0:ring] = inj[...]
    for k in range(PIECES):
        kv[1, k, :, :, LANES:] = jnp.ones((ring, rows, LANES), jnp.bfloat16)
    text_kv[1, :, LANES:] = jnp.ones((group, LANES), jnp.bfloat16)
    pl.semaphore_wait(barrier, ring - 1 + 3)

    def q_copy(k, d, many):
        there = peer(d)
        return pltpu.make_async_remote_copy(
            proj.at[0, pl.ds(k, many), :, columns(head_of(there))], queries.at[pl.ds(k, many), me],
            q_send, q_recv.at[k // 2], (e, there), MESH,
        )

    def kv_copy(k, d, many):
        there = peer(d)
        return pltpu.make_async_remote_copy(
            proj.at[pl.ds(1, 2), pl.ds(k, many), :, columns(head_of(there))],
            kv.at[:, pl.ds(k, many), me, :, pl.ds(0, LANES)],
            kv_send, kv_recv.at[k], (e, there), MESH,
        )

    def push_q(k, many):
        each(1, ring, lambda d: q_copy(k, d, many).start())
        pltpu.make_async_copy(
            proj.at[0, pl.ds(k, many), :, columns(head_of(me))],
            queries.at[pl.ds(k, many), me], q_recv.at[k // 2],
        ).start()

    def push_kv(k, many):
        each(1, ring, lambda d: kv_copy(k, d, many).start())
        pltpu.make_async_copy(
            proj.at[pl.ds(1, 2), pl.ds(k, many), :, columns(head_of(me))],
            kv.at[:, pl.ds(k, many), me, :, pl.ds(0, LANES)], kv_recv.at[k],
        ).start()

    def await_kv(k, many):
        here = kv.at[:, pl.ds(k, many), :, :, pl.ds(0, LANES)]
        pltpu.make_async_copy(here, here, kv_recv.at[k]).wait()

    def await_q(k, many):
        here = queries.at[pl.ds(k, many)]
        pltpu.make_async_copy(here, here, q_recv.at[k // 2]).wait()

    def near(distance):
        return distance - 2 * (distance // (depth - 1))

    def apart(part, odd):
        if part == 0:
            return lax.rem(z - odd + depth, depth)
        return lax.rem(2 * depth - odd - z, depth)

    def lag(part, odd):
        straight = z if part == 0 else lax.rem(depth - z, depth)
        return HOP * ((1 - half) * straight + half * (odd + 1 + near(apart(part, odd))))

    def cast_sends(part, odd):
        first, second = half == 0, half == 1
        distance = apart(part, odd)
        onward = z < depth - 1 if part == 0 else z != 1
        cross = z == odd if part == 0 else z == lax.rem(depth - odd, depth)
        back = lax.rem(z + (depth - 1) * half, depth) if part == 0 else lax.rem(z + half, depth)
        ahead = up if part == 0 else down
        return (
            (jnp.logical_or(jnp.logical_and(first, onward), jnp.logical_and(second, distance <= 1)),
             (ahead * 2 + half, me)),
            (jnp.logical_or(jnp.logical_and(first, cross), jnp.logical_and(second, distance == 0)),
             (back * 2 + 1, lax.rem(me + swap * (1 - half), ring))),
        )

    def cast_copy(k, role, part, there, first):
        here = kv.at[part, k, :, :, pl.ds(0, LANES)] if first else src.at[part, k]
        return pltpu.make_async_remote_copy(
            here, src.at[part, k], cast_send.at[2 * part + role, k],
            cast_recv.at[part, k], there, MESH,
        )

    def cast_start(k, part, odd, first):
        for role, (wanted, there) in enumerate(cast_sends(part, odd)):

            @pl.when(wanted)
            def _(role=role, there=there):
                cast_copy(k, role, part, there, first).start()

    def cast_done(k, part, odd):
        for role, (wanted, there) in enumerate(cast_sends(part, odd)):

            @pl.when(wanted)
            def _(role=role, there=there):
                cast_copy(k, role, part, there, False).wait_send()

    most = HOP * depth

    text_here = text_kv.at[:, :, pl.ds(0, LANES)]
    text_copy = pltpu.make_async_remote_copy(text, text_here, text_send, text_recv, (e, other_row), MESH)
    inj_copy = pltpu.make_async_remote_copy(inj_own, inj_here, inj_send, inj_recv, (e, other_row), MESH)


    scale = math.log2(math.e) / math.sqrt(LANES)
    usable = lax.broadcasted_iota(jnp.int32, (1, group), 1) < text_len[0]
    scores, tops = (s_a, s_b), (m_a, m_b)
    early = [PIECES] + list(range(PIECES // 2))
    late = list(range(PIECES // 2, PIECES))

    def keys_of(j):
        if j == PIECES:
            return text_kv[0, :, 0:LANES]
        return kv[0, j, :, :, 0:LANES].reshape(group, LANES)

    def values_of(j):
        if j == PIECES:
            return text_kv[1]
        return kv[1, j].reshape(group, 2 * LANES)

    def choose(k):
        for part in range(2):
            kv[part, k, :, :, 0:LANES] = jnp.where(
                mask[...] == 1,
                src[part, k].astype(jnp.float32),
                kv[part, k, :, :, 0:LANES].astype(jnp.float32),
            ).astype(jnp.bfloat16)

    def choose_two(h):
        await_kv(2 * h, 2)
        choose(2 * h)
        choose(2 * h + 1)

    def o_copy(k, d):
        there = peer(d)
        return pltpu.make_async_remote_copy(
            rows_out.at[pl.ds(k, 2), there], cols_out.at[pl.ds(k, 2), :, columns(head_of(me))],
            o_send, o_recv, (e, there), MESH,
        )

    def push_o(k):
        each(1, ring, lambda d: o_copy(k, d).start())
        pltpu.make_async_copy(
            rows_out.at[pl.ds(k, 2), me], cols_out.at[pl.ds(k, 2), :, columns(head_of(me))], o_recv
        ).start()

    def attend(chunks, i, slot, first=False, last=False):
        other = 1 - slot
        if not last:
            query = queries[i].reshape(group, LANES)
        if not first:
            before = i - 1
            top = tops[other][...]
        highest, total_out = None, None
        for place, j in enumerate(chunks):
            room = slice(place * group, (place + 1) * group)
            if not last:
                s = lax.dot_general(
                    query, keys_of(j), CONTRACT_LAST, preferred_element_type=jnp.float32
                )
                if j == PIECES:
                    s = jnp.where(usable, s, -1e30)
                scores[slot][:, room] = s
                for c in range(group // LANES):
                    part = s[:, c * LANES : (c + 1) * LANES]
                    highest = part if highest is None else jnp.maximum(highest, part)
            if not first:
                p = jnp.exp2(scores[other][:, room] * scale - top[:, 0:1]).astype(jnp.bfloat16)
                part = jnp.dot(p, values_of(j), preferred_element_type=jnp.float32)
                total_out = part if total_out is None else total_out + part
        if not last:
            found = jnp.broadcast_to(jnp.max(highest, axis=1, keepdims=True) * scale, (group, LANES))
            if chunks is late:
                found = jnp.maximum(found, early_top[i])
            tops[slot][...] = found
        if not first and chunks is early:
            early_out[before] = total_out
            early_top[before] = top
        if not first and chunks is late:
            shrink = jnp.exp2(early_top[before] - top)
            values = total_out[:, :LANES] + early_out[before, :, 0:LANES] * shrink
            weights = total_out[:, LANES:] + early_out[before, :, LANES:] * shrink
            rows_out[before] = (values / weights).astype(jnp.bfloat16).reshape(ring, rows, LANES)

    opening = PIECES + most - PIECES // 2

    def early_step(h):
        @pl.when(h == 0)
        def _():
            inj_copy.wait_recv()
            text_copy.wait_recv()

            @pl.when(jnp.logical_not(root))
            def _():
                lane = lax.broadcasted_iota(jnp.int32, (1, LANES), 1)
                for owner in range(ring):
                    taken = jnp.sum(jnp.where(lane == owner, inj_here[0:1, :], 0), axis=1, keepdims=True)
                    mask[owner] = jnp.broadcast_to(taken, (rows, LANES))
                each(0, PIECES // 4, choose_two)

            @pl.when(root)
            def _():
                await_q(0, 2)

            @pl.when(jnp.logical_not(root))
            def _():
                each(0, PIECES // 4, lambda u: await_q(4 * u, 4))

            attend(early, 0, 0, first=True)

        attend(early, 2 * h + 1, 1)

        @pl.when(h < PIECES // 2 - 1)
        def _():
            @pl.when(root)
            def _():
                await_q(2 * h + 2, 2)

            attend(early, 2 * h + 2, 0)

        @pl.when(h == PIECES // 2 - 1)
        def _():
            attend(early, PIECES, 0, last=True)

    def cast_step(t, carry):
        for odd in range(2):
            for part in range(2):
                k = t - lag(part, odd)
                here = jnp.logical_and(
                    jnp.logical_and(k >= 0, k < PIECES), lax.rem(k + 2 * most, 2) == odd
                )

                @pl.when(jnp.logical_and(here, root))
                def _(k=k, part=part, odd=odd):
                    if part == 0:
                        await_kv(k, 1)
                    cast_start(k, part, odd, True)

                @pl.when(jnp.logical_and(here, jnp.logical_not(root)))
                def _(k=k, part=part, odd=odd):
                    cast_copy(k, 0, part, (e, me), False).wait_recv()
                    cast_start(k, part, odd, False)

        @pl.when(root)
        def _():
            ahead = t + AHEAD

            @pl.when(ahead < PIECES)
            def _():
                push_kv(ahead, 1)

            @pl.when(jnp.logical_and(ahead >= PIECES, ahead < PIECES + PIECES // 2))
            def _():
                push_q(2 * (ahead - PIECES), 2)

        @pl.when(jnp.logical_not(root))
        def _():
            quick = PIECES // 4

            @pl.when(t < quick)
            def _():
                push_q(4 * t, 4)

            late_by = t - quick

            @pl.when(
                jnp.logical_and(jnp.logical_and(t >= quick, t < quick + PIECES), lax.rem(t + PIECES - quick, 2) == 0)
            )
            def _():
                push_kv(late_by, 2)

        @pl.when(t >= opening)
        def _():
            early_step(t - opening)

        return carry

    @pl.when(root)
    def _():
        each(0, AHEAD, lambda k: push_kv(k, 1))

    @pl.when(half == 1)
    def _():
        inj_copy.start()
        text_copy.start()

    @pl.when(half == 0)
    def _():
        pltpu.make_async_copy(inj_own, inj_here, inj_recv).start()
        pltpu.make_async_copy(text, text_here, text_recv).start()

    lax.fori_loop(0, PIECES + most, cast_step, 0)

    @pl.when(jnp.logical_not(root))
    def _():
        each(PIECES // 4, PIECES // 2, choose_two)

    def two(h):
        attend(late, 2 * h + 1, 1)
        attend(late, 2 * h + 2, 0)
        push_o(2 * h)

    attend(late, 0, 0, first=True)
    each(0, (PIECES - 2) // 2, two)
    attend(late, PIECES - 1, 1)
    attend(late, PIECES, 0, last=True)
    push_o(PIECES - 2)
    load_weight.wait()
    pltpu.make_async_copy(cols_out, cols_out, o_recv).wait()

    wide = 512 if out.shape[1] % 512 == 0 else LANES

    joined = cols_out[...].reshape(PIECES * rows, cols_out.shape[2])

    def project(n):
        here = pl.ds(pl.multiple_of(n * wide, wide), wide)
        result = jnp.dot(joined, weight_here[:, here], preferred_element_type=jnp.float32)
        out[:, here] = (result * gate[:, here]).astype(jnp.bfloat16)

    each(0, out.shape[1] // wide, project)

    @pl.when(half == 1)
    def _():
        inj_copy.wait_send()
        text_copy.wait_send()

    def finish_piece(k):
        for odd in range(2):

            @pl.when(lax.rem(k, 2) == odd)
            def _(odd=odd):
                for part in range(2):
                    cast_done(k, part, odd)


    each(0, PIECES, finish_piece)
    others = pl.ds(0, ring - 1)
    for sent, sem in (
        (queries.at[:, others], q_send),
        (kv.at[:, :, others, :, pl.ds(0, LANES)], kv_send),
        (rows_out.at[:, others], o_send),
    ):
        pltpu.make_async_copy(sent, sent, sem).wait()


def per_device(edits, ring, projected, inject, text_kv, text_len, out_weight, gate):
    block, width = projected.shape[1], projected.shape[3]
    rows = block // PIECES
    group = rows * ring
    half_keys = (PIECES // 2 + 1) * group
    bf16, f32, i32 = jnp.bfloat16, jnp.float32, jnp.int32
    vmem = pl.BlockSpec(memory_space=pltpu.VMEM)
    far = pl.BlockSpec(memory_space=pl.ANY)
    dma = pltpu.SemaphoreType.DMA
    result = pl.pallas_call(
        functools.partial(kernel, edits, ring),
        out_shape=jax.ShapeDtypeStruct((block, out_weight.shape[1]), bf16),
        in_specs=[far, vmem, far, pl.BlockSpec(memory_space=pltpu.SMEM), far, vmem],
        out_specs=vmem,
        scratch_shapes=[
            pltpu.VMEM((PIECES, ring, rows, LANES), bf16),
            pltpu.VMEM((2, PIECES, ring, rows, 2 * LANES), bf16),
            pltpu.VMEM((2, group, 2 * LANES), bf16),
            pltpu.VMEM((2, PIECES, ring, rows, LANES), bf16),
            pltpu.VMEM((8, LANES), i32),
            pltpu.VMEM((8, LANES), i32),
            pltpu.VMEM((ring, rows, LANES), i32),
            pltpu.VMEM((group, half_keys), f32),
            pltpu.VMEM((group, half_keys), f32),
            pltpu.VMEM((group, LANES), f32),
            pltpu.VMEM((group, LANES), f32),
            pltpu.VMEM((PIECES, ring, rows, LANES), bf16),
            pltpu.VMEM((PIECES, rows, width), bf16),
            pltpu.VMEM(out_weight.shape, bf16),
            pltpu.VMEM((PIECES, group, 2 * LANES), f32),
            pltpu.VMEM((PIECES, group, LANES), f32),
            dma, dma, dma, dma, dma, dma, dma((PIECES // 2,)),
            dma((4, PIECES)), dma((2, PIECES)), dma, dma((PIECES,)), dma, dma,
        ],
        compiler_params=pltpu.CompilerParams(
            collective_id=0, has_side_effects=True, vmem_limit_bytes=56 * 2**20
        ),
    )(
        projected[0].transpose(1, 0, 2).reshape(3, PIECES, rows, width), inject[0], text_kv[0], text_len, out_weight, gate,
    )
    return result[None]


def solution(mesh):
    return jax.shard_map(
        functools.partial(per_device, mesh.shape["edit"], mesh.shape["seq"]),
        mesh=mesh,
        in_specs=(
            P("edit", "seq", None, None),
            P("edit", "seq", None),
            P("edit", None, None, "seq"),
            P("edit"),
            P(),
            P("edit", None),
        ),
        out_specs=P("edit", "seq", None),
        check_vma=False,
    )
```

```python
import functools
import math

import jax
import jax.numpy as jnp
from jax import lax
from jax.experimental import pallas as pl
from jax.experimental.pallas import tpu as pltpu
from jax.sharding import PartitionSpec as P

MESH = pl.DeviceIdType.MESH
CONTRACT_LAST = (((1,), (1,)), ((), ()))
LANES = 128
HOP = 2
AHEAD = 3
PIECES = 16
EARLY = 8


def kernel(
    edits, ring,
    proj, inj, text, text_len, weight, gate, out,
    queries, kv, text_kv, src, inj_own, inj_here, mask, s_a, s_b, m_a, m_b, rows_out, cols_out, weight_here, shown, shown_sem,
    early_out, early_top, weight_sem, text_send, text_recv, inj_send, inj_recv, q_send, q_recv,
    cast_send, cast_recv, kv_send, kv_recv, o_send, o_recv,
):
    e = lax.axis_index("edit")
    me = lax.axis_index("seq")
    z, half = e // 2, e % 2
    depth = edits // 2
    rows = proj.shape[2]
    group = rows * ring
    root = e == 0
    swap = ring // 2
    other_row = lax.rem(me + swap, ring)

    def peer(d):
        return lax.rem(me + d, ring)

    def head_of(device):
        return lax.rem(device + swap * half, ring)

    def columns(head):
        return pl.ds(pl.multiple_of(head * LANES, LANES), LANES)

    def each(first, last, action):
        def step(d, carry):
            action(d)
            return carry

        lax.fori_loop(first, last, step, 0)

    load_weight = pltpu.make_async_copy(weight, weight_here, weight_sem)

    barrier = pltpu.get_barrier_semaphore()

    def greet(d):
        pl.semaphore_signal(barrier, inc=1, device_id=(e, peer(d)), device_id_type=MESH)

    each(1, ring, greet)
    up, down = lax.rem(z + 1, depth), lax.rem(z + depth - 1, depth)
    for other in ((up * 2 + half, me), (down * 2 + half, me), (z * 2 + 1 - half, other_row)):
        pl.semaphore_signal(barrier, inc=1, device_id=other, device_id_type=MESH)
    inj_own[...] = jnp.zeros_like(inj_own)
    inj_own[0:1, 0:ring] = inj[...]
    for k in range(PIECES):
        kv[1, k, :, :, LANES:] = jnp.ones((ring, rows, LANES), jnp.bfloat16)
    text_kv[1, :, LANES:] = jnp.ones((group, LANES), jnp.bfloat16)
    pl.semaphore_wait(barrier, ring - 1 + 3)

    def q_copy(k, d, many):
        there = peer(d)
        return pltpu.make_async_remote_copy(
            proj.at[0, pl.ds(k, many), :, columns(head_of(there))], queries.at[pl.ds(k, many), me],
            q_send, q_recv.at[k // 2], (e, there), MESH,
        )

    def kv_copy(k, d, many):
        there = peer(d)
        return pltpu.make_async_remote_copy(
            proj.at[pl.ds(1, 2), pl.ds(k, many), :, columns(head_of(there))],
            kv.at[:, pl.ds(k, many), me, :, pl.ds(0, LANES)],
            kv_send, kv_recv.at[k], (e, there), MESH,
        )

    def push_q(k, many):
        each(1, ring, lambda d: q_copy(k, d, many).start())
        pltpu.make_async_copy(
            proj.at[0, pl.ds(k, many), :, columns(head_of(me))],
            queries.at[pl.ds(k, many), me], q_recv.at[k // 2],
        ).start()

    def push_kv(k, many):
        each(1, ring, lambda d: kv_copy(k, d, many).start())
        pltpu.make_async_copy(
            proj.at[pl.ds(1, 2), pl.ds(k, many), :, columns(head_of(me))],
            kv.at[:, pl.ds(k, many), me, :, pl.ds(0, LANES)], kv_recv.at[k],
        ).start()

    def await_kv(k, many):
        here = kv.at[:, pl.ds(k, many), :, :, pl.ds(0, LANES)]
        pltpu.make_async_copy(here, here, kv_recv.at[k]).wait()

    def await_q(k, many):
        here = queries.at[pl.ds(k, many)]
        pltpu.make_async_copy(here, here, q_recv.at[k // 2]).wait()

    def near(distance):
        return distance - 2 * (distance // (depth - 1))

    def apart(part, odd):
        if part == 0:
            return lax.rem(z - odd + depth, depth)
        return lax.rem(2 * depth - odd - z, depth)

    def lag(part, odd):
        straight = z if part == 0 else lax.rem(depth - z, depth)
        return HOP * ((1 - half) * straight + half * (odd + 1 + near(apart(part, odd))))

    def cast_sends(part, odd):
        first, second = half == 0, half == 1
        distance = apart(part, odd)
        onward = z < depth - 1 if part == 0 else z != 1
        cross = z == odd if part == 0 else z == lax.rem(depth - odd, depth)
        back = lax.rem(z + (depth - 1) * half, depth) if part == 0 else lax.rem(z + half, depth)
        ahead = up if part == 0 else down
        return (
            (jnp.logical_or(jnp.logical_and(first, onward), jnp.logical_and(second, distance <= 1)),
             (ahead * 2 + half, me)),
            (jnp.logical_or(jnp.logical_and(first, cross), jnp.logical_and(second, distance == 0)),
             (back * 2 + 1, lax.rem(me + swap * (1 - half), ring))),
        )

    def cast_copy(k, role, part, there, first):
        here = kv.at[part, k, :, :, pl.ds(0, LANES)] if first else src.at[part, k]
        return pltpu.make_async_remote_copy(
            here, src.at[part, k], cast_send.at[2 * part + role, k],
            cast_recv.at[part, k], there, MESH,
        )

    def cast_start(k, part, odd, first):
        for role, (wanted, there) in enumerate(cast_sends(part, odd)):

            @pl.when(wanted)
            def _(role=role, there=there):
                cast_copy(k, role, part, there, first).start()

    def cast_done(k, part, odd):
        for role, (wanted, there) in enumerate(cast_sends(part, odd)):

            @pl.when(wanted)
            def _(role=role, there=there):
                cast_copy(k, role, part, there, False).wait_send()

    most = HOP * depth

    text_here = text_kv.at[:, :, pl.ds(0, LANES)]
    text_copy = pltpu.make_async_remote_copy(text, text_here, text_send, text_recv, (e, other_row), MESH)
    inj_copy = pltpu.make_async_remote_copy(inj_own, inj_here, inj_send, inj_recv, (e, other_row), MESH)


    scale = math.log2(math.e) / math.sqrt(LANES)
    usable = lax.broadcasted_iota(jnp.int32, (1, group), 1) < text_len[0]
    scores, tops = (s_a, s_b), (m_a, m_b)
    early = [PIECES] + list(range(EARLY))
    late = list(range(EARLY, PIECES))

    def keys_of(j):
        if j == PIECES:
            return text_kv[0, :, 0:LANES]
        return kv[0, j, :, :, 0:LANES].reshape(group, LANES)

    def values_of(j):
        if j == PIECES:
            return text_kv[1]
        return kv[1, j].reshape(group, 2 * LANES)

    def choose(k):
        for part in range(2):
            kv[part, k, :, :, 0:LANES] = jnp.where(
                mask[...] == 1,
                src[part, k].astype(jnp.float32),
                kv[part, k, :, :, 0:LANES].astype(jnp.float32),
            ).astype(jnp.bfloat16)

    def choose_two(h):
        await_kv(2 * h, 2)
        choose(2 * h)
        choose(2 * h + 1)

    def o_copy(k, d):
        there = peer(d)
        return pltpu.make_async_remote_copy(
            rows_out.at[pl.ds(k, 2), there], cols_out.at[pl.ds(k, 2), :, columns(head_of(me))],
            o_send, o_recv.at[k // (PIECES // 2)], (e, there), MESH,
        )

    def push_o(k):
        for d in range(1, ring):
            o_copy(k, d).start()
        pltpu.make_async_copy(
            rows_out.at[pl.ds(k, 2), me], cols_out.at[pl.ds(k, 2), :, columns(head_of(me))],
            o_recv.at[k // (PIECES // 2)],
        ).start()

    def attend(chunks, i, slot, first=False, last=False):
        other = 1 - slot
        if not last:
            query = queries[i].reshape(group, LANES)
        if not first:
            before = i - 1
            top = tops[other][...]
        highest, total_out = None, None
        for place, j in enumerate(chunks):
            room = slice(place * group, (place + 1) * group)
            if not last:
                s = lax.dot_general(
                    query, keys_of(j), CONTRACT_LAST, preferred_element_type=jnp.float32
                )
                if j == PIECES:
                    s = jnp.where(usable, s, -1e30)
                scores[slot][:, room] = s
                for c in range(group // LANES):
                    part = s[:, c * LANES : (c + 1) * LANES]
                    highest = part if highest is None else jnp.maximum(highest, part)
            if not first:
                p = jnp.exp2(scores[other][:, room] * scale - top[:, 0:1]).astype(jnp.bfloat16)
                part = jnp.dot(p, values_of(j), preferred_element_type=jnp.float32)
                total_out = part if total_out is None else total_out + part
        if not last:
            found = jnp.broadcast_to(jnp.max(highest, axis=1, keepdims=True) * scale, (group, LANES))
            if chunks is late:
                found = jnp.maximum(found, early_top[i])
            tops[slot][...] = found
        if not first and chunks is early:
            early_out[before] = total_out
            early_top[before] = top
        if not first and chunks is late:
            shrink = jnp.exp2(early_top[before] - top)
            values = total_out[:, :LANES] + early_out[before, :, 0:LANES] * shrink
            weights = total_out[:, LANES:] + early_out[before, :, LANES:] * shrink
            rows_out[before] = (values / weights).astype(jnp.bfloat16).reshape(ring, rows, LANES)

    last_lag = functools.reduce(jnp.maximum, [lag(part, odd) for part in range(2) for odd in range(2)])
    opening = jnp.where(root, PIECES + most - PIECES // 2, EARLY + last_lag)

    def early_step(h):
        @pl.when(h == 0)
        def _():
            inj_copy.wait_recv()
            text_copy.wait_recv()

            @pl.when(jnp.logical_not(root))
            def _():
                lane = lax.broadcasted_iota(jnp.int32, (1, LANES), 1)
                for owner in range(ring):
                    taken = jnp.sum(jnp.where(lane == owner, inj_here[0:1, :], 0), axis=1, keepdims=True)
                    mask[owner] = jnp.broadcast_to(taken, (rows, LANES))
                each(0, EARLY // 2, choose_two)

            @pl.when(root)
            def _():
                await_q(0, 2)

            @pl.when(jnp.logical_not(root))
            def _():
                each(0, PIECES // 4, lambda u: await_q(4 * u, 4))

            attend(early, 0, 0, first=True)

        attend(early, 2 * h + 1, 1)

        @pl.when(h < PIECES // 2 - 1)
        def _():
            @pl.when(root)
            def _():
                await_q(2 * h + 2, 2)

            attend(early, 2 * h + 2, 0)

        @pl.when(h == PIECES // 2 - 1)
        def _():
            attend(early, PIECES, 0, last=True)

    def cast_step(t, carry):
        share = weight.shape[0] // (PIECES // 2)

        @pl.when(jnp.logical_and(t >= PIECES // 2, t < PIECES))
        def _():
            some = pl.ds(pl.multiple_of((t - PIECES // 2) * share, share), share)
            pltpu.make_async_copy(weight.at[some], weight_here.at[some], weight_sem).start()

        for odd in range(2):
            for part in range(2):
                k = t - lag(part, odd)
                here = jnp.logical_and(
                    jnp.logical_and(k >= 0, k < PIECES), lax.rem(k + 2 * most, 2) == odd
                )

                @pl.when(jnp.logical_and(here, root))
                def _(k=k, part=part, odd=odd):
                    if part == 0:
                        await_kv(k, 1)
                    cast_start(k, part, odd, True)

                @pl.when(jnp.logical_and(here, jnp.logical_not(root)))
                def _(k=k, part=part, odd=odd):
                    cast_copy(k, 0, part, (e, me), False).wait_recv()
                    cast_start(k, part, odd, False)

        @pl.when(root)
        def _():
            ahead = t + AHEAD

            @pl.when(ahead < PIECES)
            def _():
                push_kv(ahead, 1)

            @pl.when(jnp.logical_and(ahead >= PIECES, ahead < PIECES + PIECES // 2))
            def _():
                push_q(2 * (ahead - PIECES), 2)

        @pl.when(jnp.logical_not(root))
        def _():
            quick = PIECES // 4

            @pl.when(t < quick)
            def _():
                push_q(4 * t, 4)

            late_by = t - quick

            @pl.when(
                jnp.logical_and(jnp.logical_and(t >= quick, t < quick + PIECES), lax.rem(t + PIECES - quick, 2) == 0)
            )
            def _():
                push_kv(late_by, 2)

        @pl.when(jnp.logical_and(t >= opening, t < opening + PIECES // 2))
        def _():
            early_step(t - opening)

        return carry

    @pl.when(root)
    def _():
        each(0, AHEAD, lambda k: push_kv(k, 1))

    @pl.when(half == 1)
    def _():
        inj_copy.start()
        text_copy.start()

    @pl.when(half == 0)
    def _():
        pltpu.make_async_copy(inj_own, inj_here, inj_recv).start()
        pltpu.make_async_copy(text, text_here, text_recv).start()

    lax.fori_loop(0, PIECES + most, cast_step, 0)

    @pl.when(jnp.logical_not(root))
    def _():
        each(EARLY // 2, PIECES // 2, choose_two)

    def two(h):
        push_o(2 * h - 2)
        attend(late, 2 * h + 1, 1)
        attend(late, 2 * h + 2, 0)

    attend(late, 0, 0, first=True)
    attend(late, 1, 1)
    attend(late, 2, 0)
    each(1, (PIECES - 2) // 2, two)
    push_o(PIECES - 4)
    attend(late, PIECES - 1, 1)
    attend(late, PIECES, 0, last=True)
    push_o(PIECES - 2)

    @pl.when(half == 1)
    def _():
        inj_copy.wait_send()
        text_copy.wait_send()

    def finish_piece(k):
        for odd in range(2):

            @pl.when(lax.rem(k, 2) == odd)
            def _(odd=odd):
                for part in range(2):
                    cast_done(k, part, odd)

    each(0, PIECES, finish_piece)
    others = pl.ds(0, ring - 1)
    for sent, sem in (
        (queries.at[:, others], q_send),
        (kv.at[:, :, others, :, pl.ds(0, LANES)], kv_send),
    ):
        pltpu.make_async_copy(sent, sent, sem).wait()
    load_weight.wait()

    wide = 512 if out.shape[1] % 512 == 0 else LANES
    middle = PIECES // 2
    for part in range(2):
        arrived = cols_out.at[pl.ds(part * middle, middle)]
        pltpu.make_async_copy(arrived, arrived, o_recv.at[part]).wait()
        joined = arrived[...].reshape(middle * rows, cols_out.shape[2])
        lines = pl.ds(part * middle * rows, middle * rows)

        def project(n):
            here = pl.ds(pl.multiple_of(n * wide, wide), wide)
            result = jnp.dot(joined, weight_here[:, here], preferred_element_type=jnp.float32)
            shown[lines, here] = (result * gate[:, here]).astype(jnp.bfloat16)
            pltpu.make_async_copy(shown.at[lines, here], out.at[lines, here], shown_sem).start()

        each(0, out.shape[1] // wide, project)
    pltpu.make_async_copy(rows_out.at[:, others], rows_out.at[:, others], o_send).wait()
    pltpu.make_async_copy(shown, out, shown_sem).wait()


def per_device(edits, ring, projected, inject, text_kv, text_len, out_weight, gate):
    block, width = projected.shape[1], projected.shape[3]
    rows = block // PIECES
    group = rows * ring
    half_keys = max(EARLY + 1, PIECES - EARLY) * group
    bf16, f32, i32 = jnp.bfloat16, jnp.float32, jnp.int32
    vmem = pl.BlockSpec(memory_space=pltpu.VMEM)
    far = pl.BlockSpec(memory_space=pltpu.HBM)
    dma = pltpu.SemaphoreType.DMA
    result = pl.pallas_call(
        functools.partial(kernel, edits, ring),
        out_shape=jax.ShapeDtypeStruct((block, out_weight.shape[1]), bf16),
        in_specs=[far, vmem, far, pl.BlockSpec(memory_space=pltpu.SMEM), far, vmem],
        out_specs=pl.BlockSpec(memory_space=pl.ANY),
        scratch_shapes=[
            pltpu.VMEM((PIECES, ring, rows, LANES), bf16),
            pltpu.VMEM((2, PIECES, ring, rows, 2 * LANES), bf16),
            pltpu.VMEM((2, group, 2 * LANES), bf16),
            pltpu.VMEM((2, PIECES, ring, rows, LANES), bf16),
            pltpu.VMEM((8, LANES), i32),
            pltpu.VMEM((8, LANES), i32),
            pltpu.VMEM((ring, rows, LANES), i32),
            pltpu.VMEM((group, half_keys), f32),
            pltpu.VMEM((group, half_keys), f32),
            pltpu.VMEM((group, LANES), f32),
            pltpu.VMEM((group, LANES), f32),
            pltpu.VMEM((PIECES, ring, rows, LANES), bf16),
            pltpu.VMEM((PIECES, rows, width), bf16),
            pltpu.VMEM(out_weight.shape, bf16),
            pltpu.VMEM((block, out_weight.shape[1]), bf16),
            dma,
            pltpu.VMEM((PIECES, group, 2 * LANES), f32),
            pltpu.VMEM((PIECES, group, LANES), f32),
            dma, dma, dma, dma, dma, dma, dma((PIECES // 2,)),
            dma((4, PIECES)), dma((2, PIECES)), dma, dma((PIECES,)), dma, dma((2,)),
        ],
        compiler_params=pltpu.CompilerParams(
            collective_id=0, has_side_effects=True, vmem_limit_bytes=50 * 2**20
        ),
    )(
        projected[0].transpose(1, 0, 2).reshape(3, PIECES, rows, width), inject[0], text_kv[0], text_len, out_weight, gate,
    )
    return result[None]


def solution(mesh):
    return jax.shard_map(
        functools.partial(per_device, mesh.shape["edit"], mesh.shape["seq"]),
        mesh=mesh,
        in_specs=(
            P("edit", "seq", None, None),
            P("edit", "seq", None),
            P("edit", None, None, "seq"),
            P("edit"),
            P(),
            P("edit", None),
        ),
        out_specs=P("edit", "seq", None),
        check_vma=False,
    )
```

```python
import functools
import math

import jax
import jax.numpy as jnp
from jax import lax
from jax.experimental import pallas as pl
from jax.experimental.pallas import tpu as pltpu
from jax.sharding import PartitionSpec as P

MESH = pl.DeviceIdType.MESH
CONTRACT_LAST = (((1,), (1,)), ((), ()))
LANES = 128
HOP = 2
AHEAD = 3
PIECES = 16
EARLY = 8


def kernel(
    edits, ring,
    proj, inj, text, text_len, weight, gate, out,
    queries, kv, text_kv, src, inj_own, inj_here, mask, s_a, s_b, m_a, m_b, rows_out, cols_out, weight_here, shown, shown_sem,
    early_out, early_top, weight_sem, text_send, text_recv, inj_send, inj_recv, q_send, q_recv,
    cast_send, cast_recv, kv_send, kv_recv, o_send, o_recv,
):
    e = lax.axis_index("edit")
    me = lax.axis_index("seq")
    z, half = e // 2, e % 2
    depth = edits // 2
    rows = proj.shape[2]
    group = rows * ring
    root = e == 0
    swap = ring // 2
    other_row = lax.rem(me + swap, ring)

    def peer(d):
        return lax.rem(me + d, ring)

    def head_of(device):
        return lax.rem(device + swap * half, ring)

    def columns(head):
        return pl.ds(pl.multiple_of(head * LANES, LANES), LANES)

    def each(first, last, action):
        def step(d, carry):
            action(d)
            return carry

        lax.fori_loop(first, last, step, 0)

    load_weight = pltpu.make_async_copy(weight, weight_here, weight_sem)

    barrier = pltpu.get_barrier_semaphore()

    def greet(d):
        pl.semaphore_signal(barrier, inc=1, device_id=(e, peer(d)), device_id_type=MESH)

    each(1, ring, greet)
    up, down = lax.rem(z + 1, depth), lax.rem(z + depth - 1, depth)
    for other in ((up * 2 + half, me), (down * 2 + half, me), (z * 2 + 1 - half, other_row)):
        pl.semaphore_signal(barrier, inc=1, device_id=other, device_id_type=MESH)
    inj_own[...] = jnp.zeros_like(inj_own)
    inj_own[0:1, 0:ring] = inj[...]
    for k in range(PIECES):
        kv[1, k, :, :, LANES:] = jnp.ones((ring, rows, LANES), jnp.bfloat16)
    text_kv[1, :, LANES:] = jnp.ones((group, LANES), jnp.bfloat16)
    pl.semaphore_wait(barrier, ring - 1 + 3)

    def q_copy(k, d, many):
        there = peer(d)
        return pltpu.make_async_remote_copy(
            proj.at[0, pl.ds(k, many), :, columns(head_of(there))], queries.at[pl.ds(k, many), me],
            q_send, q_recv.at[k // 2], (e, there), MESH,
        )

    def kv_copy(k, d, many):
        there = peer(d)
        return pltpu.make_async_remote_copy(
            proj.at[pl.ds(1, 2), pl.ds(k, many), :, columns(head_of(there))],
            kv.at[:, pl.ds(k, many), me, :, pl.ds(0, LANES)],
            kv_send, kv_recv.at[k], (e, there), MESH,
        )

    def push_q(k, many):
        each(1, ring, lambda d: q_copy(k, d, many).start())
        pltpu.make_async_copy(
            proj.at[0, pl.ds(k, many), :, columns(head_of(me))],
            queries.at[pl.ds(k, many), me], q_recv.at[k // 2],
        ).start()

    def push_kv(k, many):
        each(1, ring, lambda d: kv_copy(k, d, many).start())
        pltpu.make_async_copy(
            proj.at[pl.ds(1, 2), pl.ds(k, many), :, columns(head_of(me))],
            kv.at[:, pl.ds(k, many), me, :, pl.ds(0, LANES)], kv_recv.at[k],
        ).start()

    def await_kv(k, many):
        here = kv.at[:, pl.ds(k, many), :, :, pl.ds(0, LANES)]
        pltpu.make_async_copy(here, here, kv_recv.at[k]).wait()

    def await_q(k, many):
        here = queries.at[pl.ds(k, many)]
        pltpu.make_async_copy(here, here, q_recv.at[k // 2]).wait()

    def near(distance):
        return distance - 2 * (distance // (depth - 1))

    def apart(part, odd):
        if part == 0:
            return lax.rem(z - odd + depth, depth)
        return lax.rem(2 * depth - odd - z, depth)

    def lag(part, odd):
        straight = z if part == 0 else lax.rem(depth - z, depth)
        return HOP * ((1 - half) * straight + half * (odd + 1 + near(apart(part, odd))))

    def cast_sends(part, odd):
        first, second = half == 0, half == 1
        distance = apart(part, odd)
        onward = z < depth - 1 if part == 0 else z != 1
        cross = z == odd if part == 0 else z == lax.rem(depth - odd, depth)
        back = lax.rem(z + (depth - 1) * half, depth) if part == 0 else lax.rem(z + half, depth)
        ahead = up if part == 0 else down
        return (
            (jnp.logical_or(jnp.logical_and(first, onward), jnp.logical_and(second, distance <= 1)),
             (ahead * 2 + half, me)),
            (jnp.logical_or(jnp.logical_and(first, cross), jnp.logical_and(second, distance == 0)),
             (back * 2 + 1, lax.rem(me + swap * (1 - half), ring))),
        )

    def cast_copy(k, role, part, there, first):
        here = kv.at[part, k, :, :, pl.ds(0, LANES)] if first else src.at[part, k]
        return pltpu.make_async_remote_copy(
            here, src.at[part, k], cast_send.at[2 * part + role, k],
            cast_recv.at[part, k], there, MESH,
        )

    def cast_start(k, part, odd, first):
        for role, (wanted, there) in enumerate(cast_sends(part, odd)):

            @pl.when(wanted)
            def _(role=role, there=there):
                cast_copy(k, role, part, there, first).start()

    def cast_done(k, part, odd):
        for role, (wanted, there) in enumerate(cast_sends(part, odd)):

            @pl.when(wanted)
            def _(role=role, there=there):
                cast_copy(k, role, part, there, False).wait_send()

    most = HOP * depth

    text_here = text_kv.at[:, :, pl.ds(0, LANES)]
    text_copy = pltpu.make_async_remote_copy(text, text_here, text_send, text_recv, (e, other_row), MESH)
    inj_copy = pltpu.make_async_remote_copy(inj_own, inj_here, inj_send, inj_recv, (e, other_row), MESH)


    scale = math.log2(math.e) / math.sqrt(LANES)
    usable = lax.broadcasted_iota(jnp.int32, (1, group), 1) < text_len[0]
    scores, tops = (s_a, s_b), (m_a, m_b)
    early = [PIECES] + list(range(EARLY))
    late = list(range(EARLY, PIECES))

    def keys_of(j):
        if j == PIECES:
            return text_kv[0, :, 0:LANES]
        return kv[0, j, :, :, 0:LANES].reshape(group, LANES)

    def values_of(j):
        if j == PIECES:
            return text_kv[1]
        return kv[1, j].reshape(group, 2 * LANES)

    def choose(k):
        for part in range(2):
            kv[part, k, :, :, 0:LANES] = jnp.where(
                mask[...] == 1,
                src[part, k].astype(jnp.float32),
                kv[part, k, :, :, 0:LANES].astype(jnp.float32),
            ).astype(jnp.bfloat16)

    def choose_two(h):
        await_kv(2 * h, 2)
        choose(2 * h)
        choose(2 * h + 1)

    def o_copy(k, d):
        there = peer(d)
        return pltpu.make_async_remote_copy(
            rows_out.at[pl.ds(k, 2), there], cols_out.at[pl.ds(k, 2), :, columns(head_of(me))],
            o_send, o_recv.at[k // (PIECES // 2)], (e, there), MESH,
        )

    def push_o(k):
        for d in range(1, ring):
            o_copy(k, d).start()
        pltpu.make_async_copy(
            rows_out.at[pl.ds(k, 2), me], cols_out.at[pl.ds(k, 2), :, columns(head_of(me))],
            o_recv.at[k // (PIECES // 2)],
        ).start()

    def attend(chunks, i, slot, first=False, last=False):
        other = 1 - slot
        if not last:
            query = queries[i].reshape(group, LANES)
        if not first:
            before = i - 1
            top = tops[other][...]
        highest, total_out = None, None
        for place, j in enumerate(chunks):
            room = slice(place * group, (place + 1) * group)
            if not last:
                s = lax.dot_general(
                    query, keys_of(j), CONTRACT_LAST, preferred_element_type=jnp.float32
                )
                if j == PIECES:
                    s = jnp.where(usable, s, -1e30)
                scores[slot][:, room] = s
                for c in range(group // LANES):
                    part = s[:, c * LANES : (c + 1) * LANES]
                    highest = part if highest is None else jnp.maximum(highest, part)
            if not first:
                p = jnp.exp2(scores[other][:, room] * scale - top[:, 0:1]).astype(jnp.bfloat16)
                part = jnp.dot(p, values_of(j), preferred_element_type=jnp.float32)
                total_out = part if total_out is None else total_out + part
        if not last:
            found = jnp.broadcast_to(jnp.max(highest, axis=1, keepdims=True) * scale, (group, LANES))
            if chunks is late:
                found = jnp.maximum(found, early_top[i])
            tops[slot][...] = found
        if not first and chunks is early:
            early_out[before] = total_out
            early_top[before] = top
        if not first and chunks is late:
            shrink = jnp.exp2(early_top[before] - top)
            values = total_out[:, :LANES] + early_out[before, :, 0:LANES] * shrink
            weights = total_out[:, LANES:] + early_out[before, :, LANES:] * shrink
            rows_out[before] = (values / weights).astype(jnp.bfloat16).reshape(ring, rows, LANES)

    last_lag = functools.reduce(jnp.maximum, [lag(part, odd) for part in range(2) for odd in range(2)])
    opening = jnp.where(root, PIECES + most - PIECES // 2, EARLY + last_lag)

    def early_step(h):
        @pl.when(h == 0)
        def _():
            inj_copy.wait_recv()
            text_copy.wait_recv()

            @pl.when(jnp.logical_not(root))
            def _():
                lane = lax.broadcasted_iota(jnp.int32, (1, LANES), 1)
                for owner in range(ring):
                    taken = jnp.sum(jnp.where(lane == owner, inj_here[0:1, :], 0), axis=1, keepdims=True)
                    mask[owner] = jnp.broadcast_to(taken, (rows, LANES))
                each(0, EARLY // 2, choose_two)

            @pl.when(root)
            def _():
                await_q(0, 2)

            @pl.when(jnp.logical_not(root))
            def _():
                each(0, PIECES // 4, lambda u: await_q(4 * u, 4))

            attend(early, 0, 0, first=True)

        attend(early, 2 * h + 1, 1)

        @pl.when(h < PIECES // 2 - 1)
        def _():
            @pl.when(root)
            def _():
                await_q(2 * h + 2, 2)

            attend(early, 2 * h + 2, 0)

        @pl.when(h == PIECES // 2 - 1)
        def _():
            attend(early, PIECES, 0, last=True)

    def cast_step(t, carry):
        share = weight.shape[0] // (PIECES // 2)

        @pl.when(jnp.logical_and(t >= PIECES // 2, t < PIECES))
        def _():
            some = pl.ds(pl.multiple_of((t - PIECES // 2) * share, share), share)
            pltpu.make_async_copy(weight.at[some], weight_here.at[some], weight_sem).start()

        for odd in range(2):
            for part in range(2):
                k = t - lag(part, odd)
                here = jnp.logical_and(
                    jnp.logical_and(k >= 0, k < PIECES), lax.rem(k + 2 * most, 2) == odd
                )

                @pl.when(jnp.logical_and(here, root))
                def _(k=k, part=part, odd=odd):
                    if part == 0:
                        await_kv(k, 1)
                    cast_start(k, part, odd, True)

                @pl.when(jnp.logical_and(here, jnp.logical_not(root)))
                def _(k=k, part=part, odd=odd):
                    cast_copy(k, 0, part, (e, me), False).wait_recv()
                    cast_start(k, part, odd, False)

        @pl.when(root)
        def _():
            ahead = t + AHEAD

            @pl.when(ahead < PIECES)
            def _():
                push_kv(ahead, 1)

            @pl.when(jnp.logical_and(ahead >= PIECES, ahead < PIECES + PIECES // 2))
            def _():
                push_q(2 * (ahead - PIECES), 2)

        @pl.when(jnp.logical_not(root))
        def _():
            quick = PIECES // 4

            @pl.when(t < quick)
            def _():
                push_q(4 * t, 4)

            late_by = t - quick

            @pl.when(
                jnp.logical_and(jnp.logical_and(t >= quick, t < quick + PIECES), lax.rem(t + PIECES - quick, 2) == 0)
            )
            def _():
                push_kv(late_by, 2)

        @pl.when(jnp.logical_and(t >= opening, t < opening + PIECES // 2))
        def _():
            early_step(t - opening)

        return carry

    @pl.when(root)
    def _():
        each(0, AHEAD, lambda k: push_kv(k, 1))

    @pl.when(half == 1)
    def _():
        inj_copy.start()
        text_copy.start()

    @pl.when(half == 0)
    def _():
        pltpu.make_async_copy(inj_own, inj_here, inj_recv).start()
        pltpu.make_async_copy(text, text_here, text_recv).start()

    lax.fori_loop(0, PIECES + most, cast_step, 0)

    @pl.when(jnp.logical_not(root))
    def _():
        each(EARLY // 2, PIECES // 2, choose_two)

    def two(h):
        push_o(2 * h - 2)
        attend(late, 2 * h + 1, 1)
        attend(late, 2 * h + 2, 0)

    attend(late, 0, 0, first=True)
    attend(late, 1, 1)
    attend(late, 2, 0)
    each(1, (PIECES - 2) // 2, two)
    push_o(PIECES - 4)
    attend(late, PIECES - 1, 1)
    attend(late, PIECES, 0, last=True)
    push_o(PIECES - 2)

    @pl.when(half == 1)
    def _():
        inj_copy.wait_send()
        text_copy.wait_send()

    def finish_piece(k):
        for odd in range(2):

            @pl.when(lax.rem(k, 2) == odd)
            def _(odd=odd):
                for part in range(2):
                    cast_done(k, part, odd)

    each(0, PIECES, finish_piece)
    others = pl.ds(0, ring - 1)
    for sent, sem in (
        (queries.at[:, others], q_send),
        (kv.at[:, :, others, :, pl.ds(0, LANES)], kv_send),
    ):
        pltpu.make_async_copy(sent, sent, sem).wait()
    load_weight.wait()

    wide = 1024 if out.shape[1] % 1024 == 0 else LANES
    middle = PIECES // 2
    for part in range(2):
        arrived = cols_out.at[pl.ds(part * middle, middle)]
        pltpu.make_async_copy(arrived, arrived, o_recv.at[part]).wait()
        joined = arrived[...].reshape(middle * rows, cols_out.shape[2])
        lines = pl.ds(part * middle * rows, middle * rows)

        def project(n):
            here = pl.ds(pl.multiple_of(n * wide, wide), wide)
            result = jnp.dot(joined, weight_here[:, here], preferred_element_type=jnp.float32)
            shown[lines, here] = (result * gate[:, here]).astype(jnp.bfloat16)
            pltpu.make_async_copy(shown.at[lines, here], out.at[lines, here], shown_sem).start()

        each(0, out.shape[1] // wide, project)
    pltpu.make_async_copy(rows_out.at[:, others], rows_out.at[:, others], o_send).wait()
    pltpu.make_async_copy(shown, out, shown_sem).wait()


def per_device(edits, ring, projected, inject, text_kv, text_len, out_weight, gate):
    block, width = projected.shape[1], projected.shape[3]
    rows = block // PIECES
    group = rows * ring
    half_keys = max(EARLY + 1, PIECES - EARLY) * group
    bf16, f32, i32 = jnp.bfloat16, jnp.float32, jnp.int32
    vmem = pl.BlockSpec(memory_space=pltpu.VMEM)
    far = pl.BlockSpec(memory_space=pltpu.HBM)
    dma = pltpu.SemaphoreType.DMA
    result = pl.pallas_call(
        functools.partial(kernel, edits, ring),
        out_shape=jax.ShapeDtypeStruct((block, out_weight.shape[1]), bf16),
        in_specs=[far, vmem, far, pl.BlockSpec(memory_space=pltpu.SMEM), far, vmem],
        out_specs=pl.BlockSpec(memory_space=pl.ANY),
        scratch_shapes=[
            pltpu.VMEM((PIECES, ring, rows, LANES), bf16),
            pltpu.VMEM((2, PIECES, ring, rows, 2 * LANES), bf16),
            pltpu.VMEM((2, group, 2 * LANES), bf16),
            pltpu.VMEM((2, PIECES, ring, rows, LANES), bf16),
            pltpu.VMEM((8, LANES), i32),
            pltpu.VMEM((8, LANES), i32),
            pltpu.VMEM((ring, rows, LANES), i32),
            pltpu.VMEM((group, half_keys), f32),
            pltpu.VMEM((group, half_keys), f32),
            pltpu.VMEM((group, LANES), f32),
            pltpu.VMEM((group, LANES), f32),
            pltpu.VMEM((PIECES, ring, rows, LANES), bf16),
            pltpu.VMEM((PIECES, rows, width), bf16),
            pltpu.VMEM(out_weight.shape, bf16),
            pltpu.VMEM((block, out_weight.shape[1]), bf16),
            dma,
            pltpu.VMEM((PIECES, group, 2 * LANES), f32),
            pltpu.VMEM((PIECES, group, LANES), f32),
            dma, dma, dma, dma, dma, dma, dma((PIECES // 2,)),
            dma((4, PIECES)), dma((2, PIECES)), dma, dma((PIECES,)), dma, dma((2,)),
        ],
        compiler_params=pltpu.CompilerParams(
            collective_id=0, has_side_effects=True, vmem_limit_bytes=52 * 2**20
        ),
    )(
        projected[0].transpose(1, 0, 2).reshape(3, PIECES, rows, width), inject[0], text_kv[0], text_len, out_weight, gate,
    )
    return result[None]


def solution(mesh):
    return jax.shard_map(
        functools.partial(per_device, mesh.shape["edit"], mesh.shape["seq"]),
        mesh=mesh,
        in_specs=(
            P("edit", "seq", None, None),
            P("edit", "seq", None),
            P("edit", None, None, "seq"),
            P("edit"),
            P(),
            P("edit", None),
        ),
        out_specs=P("edit", "seq", None),
        check_vma=False,
    )
```
